512 devices in a mesh: dp: 2 (over core), resp: 32 (over z, x_hi), tensor: 8 (over y, x_lo).
Axes of the slice: x: 4 (x_hi: 2, x_lo: 2; x = x_hi * 2 + x_lo), y: 4, z: 16, core: 2. Of those that a mesh axis runs over, the one named last changes fastest.
Arguments:
- queries: bfloat16 [32768, 5120], P(('dp', 'resp'), 'tensor'), parts along dimension 0, may hold values from -8 to 8
- response_kv: bfloat16 [32768, 2048], P(('dp', 'resp', 'tensor')), parts along dimension 0, may hold values from -6 to 6
- prompt_kv: bfloat16 [4096, 2048], P(('dp', 'resp', 'tensor')), parts along dimension 0, may hold values from -4 to 4
- group_ids: int32 [256], P('dp'), parts along dimension 0, may hold values from 0 to 7, as said below
- lengths: int32 [256], P('dp'), parts along dimension 0, may hold values from 32 to 128
- tree_parent: int32 [256, 4], P('dp'), parts along dimension 0, may hold values from 0 to 2, as said below
Outputs:
- attended: bfloat16 [32768, 5120], P(('dp', 'resp'), 'tensor'), parts along dimension 0
The draws below stay inside these ranges and needn't reach their ends.
There are 2 independent parts, one for each index of `dp`. The reference program is written for one: setup_inputs(seed, part) draws one part's arguments, and reference() takes and returns one part's arrays. A program takes and returns all parts, laid end to end along the dimension named above; each array names one. Nothing has to cross between parts.
Inputs may be any that keep to these rules, and one draw needn't show every extreme that they name: `group_ids`: each prompt number is the prompt of exactly 16 responses. tree_parent[r, 0] = 0 and tree_parent[r, b] < b for b >= 1.
All inputs are finite; a program needn't handle non-finite values.
Results may differ from the reference program's by a relative error of at most 0.0055.
Values may be sent and summed in bfloat16 or wider, within the bound.
A program may use at most 64 MiB of HBM per device.

```python
import math
import jax
import jax.numpy as jnp
from jax import lax

H = 40
KVH = 8
HD = 128
RLEN = 128
NB = 4
PLEN = 256
RESPONSES = 128
PROMPTS = 8


def draw_queries(key, part):
    key = jax.random.fold_in(key, 11)
    first = jax.random.fold_in(key, 0)
    base = jnp.clip(jax.random.normal(first, (RESPONSES * RLEN, H * HD), jnp.float32), -4.0, 4.0)
    return base.astype(jnp.bfloat16)


def draw_prompt_kv(key, part):
    key = jax.random.fold_in(key, 23)
    first = jax.random.fold_in(key, 0)
    base = jnp.clip(jax.random.normal(first, (PROMPTS * PLEN, KVH, 2, HD), jnp.float32), -4.0, 4.0)
    return base.reshape(PROMPTS * PLEN, KVH * 2 * HD).astype(jnp.bfloat16)


def draw_group_ids(key, part):
    key = jax.random.fold_in(key, 37)
    order = jax.random.permutation(key, RESPONSES)
    return (order // 16).astype(jnp.int32)


def draw_lengths(key, part):
    key = jax.random.fold_in(key, 41)
    first, second, third = jax.random.split(key, 3)
    drawn = jax.random.randint(first, (RESPONSES,), RLEN // 4, RLEN + 1)
    longest = jax.random.randint(second, (), 0, RESPONSES)
    shortest = (longest + 1 + jax.random.randint(third, (), 0, RESPONSES - 1)) % RESPONSES
    drawn = drawn.at[longest].set(RLEN)
    drawn = drawn.at[shortest].set(RLEN // 4)
    return drawn.astype(jnp.int32)


def draw_tree_parent(key, part):
    key = jax.random.fold_in(key, 53)
    first, second = jax.random.split(key, 2)
    upper = jnp.maximum(jnp.arange(NB, dtype=jnp.int32), 1)
    drawn = jax.random.randint(first, (RESPONSES, NB), 0, upper[None, :])
    deepest = jax.random.randint(second, (), 0, RESPONSES)
    drawn = drawn.at[deepest, NB - 1].set(NB - 2)
    return drawn.astype(jnp.int32)


def block_scale(key, shape, shards, low, high):
    loudness, own = 1.0, jax.random.fold_in(key, 6)
    for axis_at, parts in shards:
        steps = jnp.exp(jax.random.uniform(jax.random.fold_in(own, axis_at), (parts,), jnp.float32, low / len(shards), high / len(shards)))
        loudness = loudness * jnp.repeat(steps, shape[axis_at] // parts).reshape([-1 if axis == axis_at else 1 for axis in range(len(shape))])
    return loudness


def gaussian(key, dims, scale, limit, pieces=(), held_as=jnp.bfloat16):
    result = scale * jax.random.normal(key, dims, jnp.float32)
    if pieces:
        result = result * block_scale(key, dims, pieces, -0.22, 0.18)
    return jnp.clip(result, -limit, limit).astype(held_as)


def setup_inputs(seed: int = 0, part: int = 0) -> dict:
    arg_keys = jax.random.split(jax.random.key(seed), 7)
    own_keys = jax.random.split(jax.random.fold_in(arg_keys[6], part), 7)
    queries = draw_queries(jax.random.fold_in(jax.random.fold_in(arg_keys[6], part), 71), part)
    response_kv = gaussian(own_keys[1], (RESPONSES * RLEN, KVH * 2 * HD), 1.0, 6.0, ((0, 256),))
    prompt_kv = draw_prompt_kv(jax.random.fold_in(jax.random.fold_in(arg_keys[6], part), 71), part)
    group_ids = draw_group_ids(jax.random.fold_in(jax.random.fold_in(arg_keys[6], part), 71), part)
    lengths = draw_lengths(jax.random.fold_in(jax.random.fold_in(arg_keys[6], part), 71), part)
    tree_parent = draw_tree_parent(jax.random.fold_in(jax.random.fold_in(arg_keys[6], part), 71), part)
    return {"queries": queries, "response_kv": response_kv, "prompt_kv": prompt_kv, "group_ids": group_ids, "lengths": lengths, "tree_parent": tree_parent}


neg_big = -1e+30

def tree_sight(parents, blocks):
    ids = jnp.arange(blocks, dtype=jnp.int32)
    step = (parents[:, :, None] == ids[None, None, :]) & (ids[None, :, None] > 0)
    sight = step
    for turn in range(blocks):
        sight = sight | jnp.any(sight[:, :, :, None] & step[:, None, :, :], axis=2)
    return sight

def reference(queries, response_kv, prompt_kv, group_ids, lengths, tree_parent):
    group = H // KVH
    width = RLEN // NB
    scale = 1.0 / math.sqrt(HD)
    sight = tree_sight(tree_parent, NB)
    q_all = queries.reshape(RESPONSES, RLEN, KVH, group, HD)
    r_all = response_kv.reshape(RESPONSES, RLEN, KVH, 2, HD)
    p_all = prompt_kv.reshape(PROMPTS, PLEN, KVH, 2, HD)
    slots = jnp.arange(RLEN, dtype=jnp.int32)
    block_of = slots // width

    def one(packed):
        query, rows, gid, length, seen = packed
        prompt = p_all[gid]
        keys = jnp.concatenate([prompt[:, :, 0], rows[:, :, 0]], 0).astype(jnp.float32)
        values = jnp.concatenate([prompt[:, :, 1], rows[:, :, 1]], 0).astype(jnp.float32)
        scores = jnp.einsum('tkgd,nkd->kgtn', query.astype(jnp.float32), keys) * scale
        same = (block_of[:, None] == block_of[None, :]) & (slots[None, :] <= slots[:, None])
        own = (same | seen[block_of[:, None], block_of[None, :]]) & (slots[None, :] < length)
        mask = jnp.concatenate([jnp.ones((RLEN, PLEN), dtype=bool), own], 1)
        masked = jnp.where(mask, scores, neg_big)
        top = lax.optimization_barrier(jnp.max(masked, axis=-1, keepdims=True))
        weights = jnp.where(mask, jnp.exp(scores - top), 0.0)
        total = lax.optimization_barrier(jnp.sum(weights, axis=-1))
        rounded = lax.optimization_barrier(weights.astype(jnp.bfloat16)).astype(jnp.float32)
        acc = jnp.einsum('kgtn,nkd->kgtd', rounded, values)
        out = (acc / total[..., None]).transpose(2, 0, 1, 3)
        out = jnp.where((slots < length)[:, None, None, None], out, 0.0)
        return out.reshape(RLEN, H * HD).astype(jnp.bfloat16)
    outs = lax.map(one, (q_all, r_all, group_ids, lengths, sight))
    return outs.reshape(RESPONSES * RLEN, H * HD)
```

```python
import functools
import math

import jax
import jax.numpy as jnp
from jax import lax
from jax.experimental import pallas as pl
from jax.experimental.pallas import tpu as pltpu
from jax.sharding import PartitionSpec as P

H = 40
KVH = 8
HD = 128
RLEN = 128
NB = 4
PLEN = 256
GROUP = H // KVH
RESP_DEV = 4
WIDTH = RLEN // NB
NZ = 16
SLOTS = 16
LINE = 8
NEG = -1e30
C2 = math.log2(math.e) / math.sqrt(HD)
MESH = pl.DeviceIdType.MESH
STEPS = (((0, 3), (0, 1)), ((3, 6), (3, 4), (3, 2)), ((6, 8), (6, 7), (6, 5)))
REACH = sorted({c - p for step in STEPS for p, c in step} | {p - c for step in STEPS for p, c in step})


def half(kv, sign, c):
    return c != 8 or (sign == 1) == (kv == 0)


def own_mask(first, j, lengths, parents):
    length = lengths[first + j]
    p2 = parents[2, first + j]
    p3 = parents[3, first + j]
    s21 = p2 == 1
    s32 = p3 == 2
    s31 = (p3 == 1) | (s32 & s21)
    row = lax.broadcasted_iota(jnp.int32, (RLEN, RLEN), 0)
    col = lax.broadcasted_iota(jnp.int32, (RLEN, RLEN), 1)
    rb = row // WIDTH
    cb = col // WIDTH
    reach = jnp.where(rb == cb, row, -1)
    reach = jnp.where((cb == 0) & (rb > 0), RLEN, reach)
    reach = jnp.where((cb == 1) & (rb == 2), jnp.where(s21, RLEN, -1), reach)
    reach = jnp.where((cb == 1) & (rb == 3), jnp.where(s31, RLEN, -1), reach)
    reach = jnp.where((cb == 2) & (rb == 3), jnp.where(s32, RLEN, -1), reach)
    return (col <= reach) & (col < length)


def kernel(
    q_hbm, r_hbm, p_hbm, gids, lengths, parents, out_hbm,
    qs, kb, vb, rb, acc_s, m_s, p_s, obuf,
    lsem, asend, arecv, rsend, rrecv, zsend, zrecv, qsem, osem,
):
    resp = lax.axis_index("resp")
    t = lax.axis_index("tensor")
    z = resp // 2
    xh = resp % 2
    first = resp * RESP_DEV
    bufs = (kb, vb)

    def zz(o):
        return (z + o + NZ) % NZ

    def remote(src, dst, ss, rs, r, tt):
        return pltpu.make_async_remote_copy(
            src_ref=src, dst_ref=dst, send_sem=ss, recv_sem=rs,
            device_id={"resp": r, "tensor": tt}, device_id_type=MESH,
        )

    q_copy = pltpu.make_async_copy(q_hbm, qs, qsem)
    q_copy.start()

    peers = [(k // 8, k % 8) for k in range(1, SLOTS)]
    barrier = pltpu.get_barrier_semaphore()
    for o in REACH:
        pl.semaphore_signal(barrier, inc=1, device_id={"resp": zz(o) * 2 + xh, "tensor": t}, device_id_type=MESH)
    for dx, dt in peers:
        pl.semaphore_signal(
            barrier, inc=1, device_id={"resp": z * 2 + (xh + dx) % 2, "tensor": (t + dt) % 8}, device_id_type=MESH
        )
    pl.semaphore_wait(barrier, len(REACH) + len(peers))

    slot = xh * 8 + t

    def cols(tt, kv):
        return pl.ds(pl.multiple_of(tt * (2 * HD) + kv * HD, HD), HD)

    def pair(tt):
        return pl.ds(pl.multiple_of(tt * (2 * HD), 2 * HD), 2 * HD)

    def own_prompt(kv):
        return pltpu.make_async_copy(p_hbm.at[:, cols(t, kv)], bufs[kv].at[z, slot], lsem.at[kv])

    for kv in range(2):
        for dx, dt in peers:
            tt = (t + dt) % 8
            remote(
                p_hbm.at[:, cols(tt, kv)], bufs[kv].at[z, slot], asend.at[kv], arecv.at[kv], z * 2 + (xh + dx) % 2, tt
            ).start()
        own_prompt(kv).start()

    def own_rows():
        return pltpu.make_async_copy(r_hbm.at[:, pair(t)], rb.at[t], lsem.at[2])

    def rows_to(dt):
        tt = (t + dt) % 8
        return remote(r_hbm.at[:, pair(tt)], rb.at[t], rsend, rrecv, resp, tt)

    own_rows().start()
    for dt in range(1, 8):
        rows_to(dt).start()

    def hop(kv, sign, p, c):
        ref = bufs[kv].at[zz(-sign * p)]
        return remote(ref, ref, zsend.at[kv, sign % 3, c], zrecv.at[kv, sign % 3, c], zz(sign * (c - p)) * 2 + xh, t)

    started = []
    arrived = set()

    def arrive(kv, sign, c):
        if c == 0:
            sign = 0
        if (kv, sign, c) in arrived:
            return
        arrived.add((kv, sign, c))
        if c == 0:
            own_prompt(kv).wait()
            ref = bufs[kv].at[z, pl.ds(0, SLOTS - 1)]
            pltpu.make_async_copy(ref, ref, arecv.at[kv]).wait()
        else:
            hop(kv, sign, 0, c).wait_recv()

    def forward(kv, step):
        for p, c in STEPS[step]:
            for sign in (1, -1):
                if half(kv, sign, c):
                    arrive(kv, sign, p)
                    hop(kv, sign, p, c).start()
                    started.append((kv, sign, p, c))

    forward(0, 0)
    forward(1, 0)

    ref = rb.at[pl.ds(0, 7)]
    own_rows().wait()
    pltpu.make_async_copy(ref, ref, rrecv).wait()
    q_copy.wait()
    ones = jnp.ones((RLEN, HD), jnp.bfloat16)

    def own_part(j, carry):
        rows = rb[pl.ds(2 * j, 2)].reshape(RLEN, 2 * HD)
        keys = rows[:, :HD]
        values = jnp.concatenate([rows[:, HD:], ones], axis=1)
        mask = own_mask(first, j, lengths, parents)
        for g in range(GROUP):
            query = qs[pl.ds(j * RLEN, RLEN), g * HD : (g + 1) * HD]
            s = lax.dot_general(query, keys, (((1,), (1,)), ((), ())), preferred_element_type=jnp.float32)
            s = jnp.where(mask, s, NEG)
            m = jnp.max(s, axis=1, keepdims=True)
            e = jnp.exp2(s * C2 - m * C2).astype(jnp.bfloat16)
            acc_s[j, g] = jnp.dot(e, values, preferred_element_type=jnp.float32)
            m_s[j, g] = jnp.broadcast_to(m, (RLEN, HD))
        return carry

    lax.fori_loop(0, RESP_DEV, own_part, 0)

    forward(0, 1)
    forward(1, 1)
    forward(0, 2)
    forward(1, 2)

    for kv, sign, p, c in started:
        if kv == 0:
            arrive(kv, sign, c)

    def chosen(buf, j):
        gid = gids[first + j]
        rows = buf[pl.ds(2 * gid, 2)]
        return rows.astype(jnp.float32).reshape(PLEN, HD).astype(jnp.bfloat16)

    def prompt_keys(j, carry):
        keys = chosen(kb, j)
        for g in range(GROUP):
            query = qs[pl.ds(j * RLEN, RLEN), g * HD : (g + 1) * HD]
            s = lax.dot_general(query, keys, (((1,), (1,)), ((), ())), preferred_element_type=jnp.float32)
            m_own = m_s[j, g]
            m = jnp.maximum(m_own, jnp.max(s, axis=1, keepdims=True))
            mc = m * C2
            factor = jnp.exp2(m_own * C2 - mc)
            acc_s[j, g] = acc_s[j, g] * jnp.concatenate([factor, factor], axis=1)
            e = jnp.exp2(s * C2 - jnp.concatenate([mc, mc], axis=1))
            p_s[j, g] = e.astype(jnp.bfloat16)
        return carry

    lax.fori_loop(0, RESP_DEV, prompt_keys, 0)

    for kv, sign, p, c in started:
        if kv == 1:
            arrive(kv, sign, c)

    wide = jnp.ones((PLEN, HD), jnp.bfloat16)

    def prompt_values(j, carry):
        values = jnp.concatenate([chosen(vb, j), wide], axis=1)
        live = lax.broadcasted_iota(jnp.int32, (RLEN, HD), 0) < lengths[first + j]
        for g in range(GROUP):
            acc = acc_s[j, g] + jnp.dot(p_s[j, g], values, preferred_element_type=jnp.float32)
            o = jnp.where(live, acc[:, :HD] / acc[:, HD:], 0.0)
            obuf[pl.ds(j * RLEN, RLEN), g * HD : (g + 1) * HD] = o.astype(jnp.bfloat16)
        return carry

    lax.fori_loop(0, RESP_DEV, prompt_values, 0)
    o_copy = pltpu.make_async_copy(obuf, out_hbm, osem)
    o_copy.start()

    for kv, sign, p, c in started:
        hop(kv, sign, p, c).wait_send()
    for kv in range(2):
        ref = bufs[kv].at[z, pl.ds(0, SLOTS - 1)]
        pltpu.make_async_copy(ref, ref, asend.at[kv]).wait()
    ref = rb.at[pl.ds(0, 7)]
    pltpu.make_async_copy(ref, ref, rsend).wait()
    o_copy.wait()


def local(queries, response_kv, prompt_kv, group_ids, lengths, tree_parent):
    dma = pltpu.SemaphoreType.DMA
    anywhere = pl.BlockSpec(memory_space=pl.ANY)
    scalars = pl.BlockSpec(memory_space=pltpu.SMEM)
    return pl.pallas_call(
        kernel,
        out_shape=jax.ShapeDtypeStruct(queries.shape, jnp.bfloat16),
        in_specs=[anywhere, anywhere, anywhere, scalars, scalars, scalars],
        out_specs=anywhere,
        scratch_shapes=[
            pltpu.VMEM((RESP_DEV * RLEN, GROUP * HD), jnp.bfloat16),
            pltpu.VMEM((NZ, SLOTS, LINE, HD), jnp.bfloat16),
            pltpu.VMEM((NZ, SLOTS, LINE, HD), jnp.bfloat16),
            pltpu.VMEM((8, 64, 2 * HD), jnp.bfloat16),
            pltpu.VMEM((RESP_DEV, GROUP, RLEN, 2 * HD), jnp.float32),
            pltpu.VMEM((RESP_DEV, GROUP, RLEN, HD), jnp.float32),
            pltpu.VMEM((RESP_DEV, GROUP, RLEN, PLEN), jnp.bfloat16),
            pltpu.VMEM((RESP_DEV * RLEN, GROUP * HD), jnp.bfloat16),
            dma((3,)), dma((2,)), dma((2,)), dma, dma, dma((2, 3, 9)), dma((2, 3, 9)), dma, dma,
        ],
        compiler_params=pltpu.CompilerParams(
            collective_id=0, has_side_effects=True, vmem_limit_bytes=60 << 20
        ),
        cost_estimate=pl.CostEstimate(flops=1 << 29, bytes_accessed=3 << 20, transcendentals=1 << 20),
    )(queries, response_kv, prompt_kv, group_ids, lengths, tree_parent.T)


def solution(mesh):
    placed = (
        P(("dp", "resp"), "tensor"),
        P(("dp", "resp", "tensor"), None),
        P(("dp", "resp", "tensor"), None),
        P("dp"),
        P("dp"),
        P("dp", None),
    )
    return jax.shard_map(
        local, mesh=mesh, in_specs=placed, out_specs=P(("dp", "resp"), "tensor"), check_vma=False
    )
```

```python
import math

import jax
import jax.numpy as jnp
from jax import lax
from jax.experimental import pallas as pl
from jax.experimental.pallas import tpu as pltpu
from jax.sharding import PartitionSpec as P

H = 40
KVH = 8
HD = 128
RLEN = 128
NB = 4
PLEN = 256
RESPONSES = 128
GROUP = H // KVH
RESP_DEV = 4
NZ = 16
SLOTS = 16
LINE = 8
NEG = -1e30
C2 = math.log2(math.e) / math.sqrt(HD)
MESH = pl.DeviceIdType.MESH
STEPS = (((0, 3),), ((3, 6),))
AHEAD = 6
NEAR = (3, -3, 2, -2, 1, -1)


def own_mask(first, j, lengths, parents):
    length = lengths[first + j]
    p2 = parents[2, first + j]
    p3 = parents[3, first + j]
    s21 = p2 == 1
    s32 = p3 == 2
    s31 = (p3 == 1) | (s32 & s21)
    row = lax.broadcasted_iota(jnp.int32, (RLEN, RLEN), 0)
    col = lax.broadcasted_iota(jnp.int32, (RLEN, RLEN), 1)
    rb = row >> 5
    cb = col >> 5
    reach = jnp.where(rb == cb, row, -1)
    reach = jnp.where((cb == 0) & (rb > 0), RLEN, reach)
    reach = jnp.where((cb == 1) & (rb == 2), jnp.where(s21, RLEN, -1), reach)
    reach = jnp.where((cb == 1) & (rb == 3), jnp.where(s31, RLEN, -1), reach)
    reach = jnp.where((cb == 2) & (rb == 3), jnp.where(s32, RLEN, -1), reach)
    return (col <= reach) & (col < length)


def kernel(
    q_hbm, r_hbm, p_hbm, g_hbm, l_hbm, t_hbm, obuf,
    gids, lengths, parents, qs, raw, prompts, rb, acc_s, m_s,
    psend, precv, rsend, rrecv, zsend, zrecv, qsem, ssem, lsem, ready,
):
    resp = lax.axis_index("resp")
    t = lax.axis_index("tensor")
    z = resp // 2
    xh = resp % 2
    first = resp * RESP_DEV
    slot = xh * 8 + t

    def zz(o):
        return (z + o + NZ) % NZ

    def place(r, tt):
        return {"resp": r, "tensor": tt}

    def remote(src, dst, ss, rs, r, tt):
        return pltpu.make_async_remote_copy(
            src_ref=src, dst_ref=dst, send_sem=ss, recv_sem=rs, device_id=place(r, tt), device_id_type=MESH
        )

    peers = sorted(
        ((k // 8, k % 8) for k in range(1, SLOTS)), key=lambda p: (-2 * p[0] - min(p[1] // 2, 4 - p[1] // 2) - p[1] % 2, p)
    )

    def greet(sem, r, tt):
        pl.semaphore_signal(sem, inc=1, device_id=place(r, tt), device_id_type=MESH)

    barrier = pltpu.get_barrier_semaphore()
    for o in NEAR:
        greet(barrier, zz(o) * 2 + xh, t)
    for dx, dt in peers:
        greet(barrier, z * 2 + (xh + dx) % 2, (t + dt) % 8)

    own_raw = pltpu.make_async_copy(p_hbm, raw.at[z], lsem)
    own_raw.start()
    small = [
        pltpu.make_async_copy(src, dst, ssem.at[i])
        for i, (src, dst) in enumerate(((g_hbm, gids), (l_hbm, lengths), (t_hbm, parents)))
    ]
    for copy in small:
        copy.start()
    q_copy = pltpu.make_async_copy(q_hbm, qs, qsem)
    q_copy.start()

    own_raw.wait()
    pl.semaphore_wait(barrier, len(NEAR) + len(peers))

    def pair(tt):
        return pl.ds(pl.multiple_of(tt * (2 * HD), 2 * HD), 2 * HD)

    started = []
    here = set()
    waiting = []

    def hop(sign, p, c):
        ref = raw.at[zz(-sign * p)]
        return remote(ref, ref, zsend.at[sign % 3, c], zrecv.at[sign % 3, c], zz(sign * (c - p)) * 2 + xh, t)

    def arrive(sign, c):
        sign = sign if c else 0
        if (sign, c) not in here:
            here.add((sign, c))
            if c:
                hop(sign, 0, c).wait_recv()
            waiting.append((sign, c))

    def forward(step):
        for p, c in STEPS[step]:
            for sign in (1, -1):
                if c != 8 or sign == 1:
                    arrive(sign, p)
                    hop(sign, p, c).start()
                    started.append((sign, p, c))

    spread_count = [0]

    def to_plane(src, o, half=None):
        targets = peers if o == 0 else peers + [(0, 0)]
        for dx, dt in targets:
            if half is not None and dx:
                continue
            tt = (t + dt) % 8
            r = zz(o) * 2 + (half if half is not None else (xh + dx) % 2)
            remote(raw.at[src, :, pair(tt)], prompts.at[src, slot], psend, precv, r, tt).start()
            spread_count[0] += 1
        if o == 0:
            pltpu.make_async_copy(raw.at[src, :, pair(t)], prompts.at[src, slot], precv).start()

    def spread():
        while waiting:
            sign, c = waiting.pop(0)
            src = zz(-sign * c)
            if c == AHEAD:
                to_plane(src, 2 * sign, 0 if sign == 1 else 1)
            to_plane(src, 1)
            to_plane(src, -1)
            to_plane(src, 0)

    arrive(0, 0)
    forward(0)
    for dx, dt in peers:
        greet(ready, z * 2 + (xh + dx) % 2, (t + dt) % 8)
    waiting.clear()
    to_plane(z, 0)

    pltpu.make_async_copy(r_hbm.at[:, pair(t)], rb.at[t], rrecv).start()
    for dt in range(1, 8):
        tt = (t + dt) % 8
        remote(r_hbm.at[:, pair(tt)], rb.at[t], rsend, rrecv, resp, tt).start()

    pl.semaphore_wait(ready, len(peers))
    to_plane(z, 1)
    to_plane(z, -1)

    for copy in small:
        copy.wait()
    q_copy.wait()

    def stacked(j):
        rows = qs[pl.ds(j * RLEN, RLEN), :]
        return jnp.concatenate([rows[:, g * HD : (g + 1) * HD] for g in range(GROUP)], axis=0)

    def own_part(j, carry):
        rows = rb[pl.ds(2 * j, 2)].reshape(RLEN, 2 * HD)
        keys = rows[:, :HD]
        values = jnp.concatenate([rows[:, HD:], jnp.ones((RLEN, HD), jnp.bfloat16)], axis=1)
        bias = jnp.where(own_mask(first, j, lengths, parents), 0.0, NEG)
        s = lax.dot_general(stacked(j), keys, (((1,), (1,)), ((), ())), preferred_element_type=jnp.float32)
        s = s + jnp.concatenate([bias] * GROUP, axis=0)
        m = jnp.max(s, axis=1, keepdims=True)
        e = jnp.exp2(s * C2 - m * C2).astype(jnp.bfloat16)
        acc_s[j] = jnp.dot(e, values, preferred_element_type=jnp.float32)
        m_s[j] = jnp.broadcast_to(m, (GROUP * RLEN, HD))
        return carry

    def own():
        pltpu.make_async_copy(rb, rb, rrecv).wait()
        lax.fori_loop(0, RESP_DEV, own_part, 0)

    for step in range(1, len(STEPS)):
        forward(step)
        spread()
    for sign, p, c in started:
        arrive(sign, c)
        spread()
    own()
    pltpu.make_async_copy(prompts, prompts, precv).wait()

    def chosen(j, at):
        rows = prompts[pl.ds(2 * gids[first + j], 2), :, :, at : at + HD]
        return rows.astype(jnp.float32).reshape(PLEN, HD).astype(jnp.bfloat16)

    def prompt_part(j, carry):
        s = lax.dot_general(stacked(j), chosen(j, 0), (((1,), (1,)), ((), ())), preferred_element_type=jnp.float32)
        m_own = m_s[j]
        m = jnp.maximum(m_own, jnp.max(s, axis=1, keepdims=True))
        mc = m * C2
        factor = jnp.exp2(m_own * C2 - mc)
        e = jnp.exp2(s * C2 - jnp.concatenate([mc, mc], axis=1)).astype(jnp.bfloat16)
        values = jnp.concatenate([chosen(j, HD), jnp.ones((PLEN, HD), jnp.bfloat16)], axis=1)
        acc = acc_s[j] * jnp.concatenate([factor, factor], axis=1)
        acc = acc + jnp.dot(e, values, preferred_element_type=jnp.float32)
        o = acc[:, :HD] / acc[:, HD:]
        live = lax.broadcasted_iota(jnp.int32, (RLEN, HD), 0) < lengths[first + j]
        for g in range(GROUP):
            part = jnp.where(live, o[g * RLEN : (g + 1) * RLEN], 0.0)
            obuf[pl.ds(j * RLEN, RLEN), g * HD : (g + 1) * HD] = part.astype(jnp.bfloat16)
        return carry

    lax.fori_loop(0, RESP_DEV, prompt_part, 0)
    for sign, p, c in started:
        hop(sign, p, c).wait_send()
    left = spread_count[0]
    while left:
        n = min(left, NZ * SLOTS)
        left -= n
        if n >= SLOTS:
            pltpu.make_async_copy(
                prompts.at[pl.ds(0, n // SLOTS)], prompts.at[pl.ds(0, n // SLOTS)], psend
            ).wait()
        if n % SLOTS:
            ref = prompts.at[0, pl.ds(0, n % SLOTS)]
            pltpu.make_async_copy(ref, ref, psend).wait()
    ref = rb.at[pl.ds(0, 7)]
    pltpu.make_async_copy(ref, ref, rsend).wait()


def store(src, dst, sem):
    copy = pltpu.make_async_copy(src, dst, sem)
    copy.start()
    copy.wait()


def local(queries, response_kv, prompt_kv, group_ids, lengths, tree_parent):
    dma = pltpu.SemaphoreType.DMA
    anywhere = pl.BlockSpec(memory_space=pl.ANY)
    attended = pl.pallas_call(
        kernel,
        out_shape=pltpu.VMEM(queries.shape, jnp.bfloat16),
        in_specs=[anywhere] * 6,
        out_specs=pl.BlockSpec(memory_space=pltpu.VMEM),
        scratch_shapes=[
            pltpu.SMEM((RESPONSES,), jnp.int32),
            pltpu.SMEM((RESPONSES,), jnp.int32),
            pltpu.SMEM((NB, RESPONSES), jnp.int32),
            pltpu.VMEM((RESP_DEV * RLEN, GROUP * HD), jnp.bfloat16),
            pltpu.VMEM((NZ, LINE, KVH * 2 * HD), jnp.bfloat16),
            pltpu.VMEM((NZ, SLOTS, LINE, 2 * HD), jnp.bfloat16),
            pltpu.VMEM((8, 64, 2 * HD), jnp.bfloat16),
            pltpu.VMEM((RESP_DEV, GROUP * RLEN, 2 * HD), jnp.float32),
            pltpu.VMEM((RESP_DEV, GROUP * RLEN, HD), jnp.float32),
            dma, dma, dma, dma, dma((3, 9)), dma((3, 9)), dma, dma((3,)), dma, pltpu.SemaphoreType.REGULAR,
        ],
        compiler_params=pltpu.CompilerParams(
            collective_id=0, has_side_effects=True, vmem_limit_bytes=60 << 20
        ),
        cost_estimate=pl.CostEstimate(flops=1 << 29, bytes_accessed=3 << 20, transcendentals=1 << 20),
    )(queries, response_kv, prompt_kv, group_ids, lengths, tree_parent.T)
    return pl.pallas_call(
        store,
        out_shape=jax.ShapeDtypeStruct(queries.shape, jnp.bfloat16),
        in_specs=[pl.BlockSpec(memory_space=pltpu.VMEM)],
        out_specs=anywhere,
        scratch_shapes=[dma],
        compiler_params=pltpu.CompilerParams(vmem_limit_bytes=2 << 20),
    )(attended)


def solution(mesh):
    placed = (
        P(("dp", "resp"), "tensor"),
        P(("dp", "resp", "tensor"), None),
        P(("dp", "resp", "tensor"), None),
        P("dp"),
        P("dp"),
        P("dp", None),
    )
    return jax.shard_map(
        local, mesh=mesh, in_specs=placed, out_specs=P(("dp", "resp"), "tensor"), check_vma=False
    )
```

```python
import math

import jax
import jax.numpy as jnp
from jax import lax
from jax.experimental import pallas as pl
from jax.experimental.pallas import tpu as pltpu
from jax.sharding import PartitionSpec as P

H = 40
KVH = 8
HD = 128
RLEN = 128
NB = 4
PLEN = 256
RESPONSES = 128
GROUP = H // KVH
RESP_DEV = 4
NZ = 16
SLOTS = 16
LINE = 8
NEG = -1e30
C2 = math.log2(math.e) / math.sqrt(HD)
MESH = pl.DeviceIdType.MESH
NEAR = (3, -3, 2, -2, 1, -1)


def own_mask(first, j, lengths, parents):
    length = lengths[first + j]
    p2 = parents[2, first + j]
    p3 = parents[3, first + j]
    s21 = p2 == 1
    s32 = p3 == 2
    s31 = (p3 == 1) | (s32 & s21)
    row = lax.broadcasted_iota(jnp.int32, (RLEN, RLEN), 0)
    col = lax.broadcasted_iota(jnp.int32, (RLEN, RLEN), 1)
    rb = row >> 5
    cb = col >> 5
    reach = jnp.where(rb == cb, row, -1)
    reach = jnp.where((cb == 0) & (rb > 0), RLEN, reach)
    reach = jnp.where((cb == 1) & (rb == 2), jnp.where(s21, RLEN, -1), reach)
    reach = jnp.where((cb == 1) & (rb == 3), jnp.where(s31, RLEN, -1), reach)
    reach = jnp.where((cb == 2) & (rb == 3), jnp.where(s32, RLEN, -1), reach)
    return (col <= reach) & (col < length)


def kernel(
    q_hbm, r_hbm, p_hbm, g_hbm, l_hbm, t_hbm, obuf,
    gids, lengths, parents, qs, kr, vr, kb, vb, rb, acc_s, m_s, p_s,
    psend, precv, rsend, rrecv, zsend, zrecv, qsem, ssem, lsem, ready,
):
    resp = lax.axis_index("resp")
    t = lax.axis_index("tensor")
    z = resp // 2
    xh = resp % 2
    first = resp * RESP_DEV
    slot = xh * 8 + t

    def zz(o):
        return (z + o + NZ) % NZ

    def place(r, tt):
        return {"resp": r, "tensor": tt}

    def remote(src, dst, ss, rs, r, tt):
        return pltpu.make_async_remote_copy(
            src_ref=src, dst_ref=dst, send_sem=ss, recv_sem=rs, device_id=place(r, tt), device_id_type=MESH
        )

    peers = sorted(
        ((k // 8, k % 8) for k in range(1, SLOTS)), key=lambda p: (-2 * p[0] - min(p[1] // 2, 4 - p[1] // 2) - p[1] % 2, p)
    )

    def greet(sem, r, tt):
        pl.semaphore_signal(sem, inc=1, device_id=place(r, tt), device_id_type=MESH)

    barrier = pltpu.get_barrier_semaphore()
    for o in NEAR:
        greet(barrier, zz(o) * 2 + xh, t)
    for dx, dt in peers:
        greet(barrier, z * 2 + (xh + dx) % 2, (t + dt) % 8)

    raws = (kr, vr)
    for kv in range(2):
        for h in range(KVH):
            pltpu.make_async_copy(
                p_hbm.at[:, pl.ds((2 * h + kv) * HD, HD)], raws[kv].at[z, :, pl.ds(h * HD, HD)], lsem.at[kv]
            ).start()
    small = [
        pltpu.make_async_copy(src, dst, ssem.at[i])
        for i, (src, dst) in enumerate(((g_hbm, gids), (l_hbm, lengths), (t_hbm, parents)))
    ]
    for copy in small:
        copy.start()
    q_copy = pltpu.make_async_copy(q_hbm, qs, qsem)
    q_copy.start()

    for kv in range(2):
        pltpu.make_async_copy(raws[kv].at[z], raws[kv].at[z], lsem.at[kv]).wait()
    pl.semaphore_wait(barrier, len(NEAR) + len(peers))

    def pair(tt):
        return pl.ds(pl.multiple_of(tt * (2 * HD), 2 * HD), 2 * HD)

    def hop(kv, sign, p, c):
        ref = raws[kv].at[zz(-sign * p)]
        return remote(
            ref, ref, zsend.at[kv, sign % 3, c], zrecv.at[kv, sign % 3, c], zz(sign * (c - p)) * 2 + xh, t
        )

    def forward(kv, p, c):
        for sign in (1, -1):
            if p:
                hop(kv, sign, 0, p).wait_recv()
            hop(kv, sign, p, c).start()

    spread_count = [0]

    def column(tt):
        return pl.ds(pl.multiple_of(tt * HD, HD), HD)

    def to_plane(src, o, half=None, kvs=(0, 1)):
        targets = peers if o == 0 else peers + [(0, 0)]
        for kv in kvs:
            buf = (kb, vb)[kv]
            for dx, dt in targets:
                if half is not None and dx:
                    continue
                tt = (t + dt) % 8
                r = zz(o) * 2 + (half if half is not None else (xh + dx) % 2)
                remote(raws[kv].at[src, :, column(tt)], buf.at[src, slot], psend.at[kv], precv.at[kv], r, tt).start()
                if kv == 0:
                    spread_count[0] += 1
            if o == 0:
                pltpu.make_async_copy(raws[kv].at[src, :, column(t)], buf.at[src, slot], precv.at[kv]).start()

    def spread(kv, c):
        for sign in (1, -1):
            src = zz(-c * sign)
            if c == 6:
                to_plane(src, 2 * sign, 0 if sign == 1 else 1, (kv,))
            for o in (1, -1, 0):
                to_plane(src, o, None, (kv,))

    forward(0, 0, 3)
    forward(1, 0, 3)
    for dx, dt in peers:
        greet(ready, z * 2 + (xh + dx) % 2, (t + dt) % 8)
    to_plane(z, 0)

    pltpu.make_async_copy(r_hbm.at[:, pair(t)], rb.at[t], rrecv).start()
    for dt in range(1, 8):
        tt = (t + dt) % 8
        remote(r_hbm.at[:, pair(tt)], rb.at[t], rsend, rrecv, resp, tt).start()

    pl.semaphore_wait(ready, len(peers))
    to_plane(z, 1)
    to_plane(z, -1)

    for copy in small:
        copy.wait()
    q_copy.wait()

    def stacked(j):
        rows = qs[pl.ds(j * RLEN, RLEN), :]
        return jnp.concatenate([rows[:, g * HD : (g + 1) * HD] for g in range(GROUP)], axis=0)

    def own_part(j, carry):
        rows = rb[pl.ds(2 * j, 2)].reshape(RLEN, 2 * HD)
        keys = rows[:, :HD]
        values = jnp.concatenate([rows[:, HD:], jnp.ones((RLEN, HD), jnp.bfloat16)], axis=1)
        bias = jnp.where(own_mask(first, j, lengths, parents), 0.0, NEG)
        s = lax.dot_general(stacked(j), keys, (((1,), (1,)), ((), ())), preferred_element_type=jnp.float32)
        s = s + jnp.concatenate([bias] * GROUP, axis=0)
        m = jnp.max(s, axis=1, keepdims=True)
        e = jnp.exp2(s * C2 - m * C2).astype(jnp.bfloat16)
        acc_s[j] = jnp.dot(e, values, preferred_element_type=jnp.float32)
        m_s[j] = jnp.broadcast_to(m, (GROUP * RLEN, HD))
        return carry

    def own():
        pltpu.make_async_copy(rb, rb, rrecv).wait()
        lax.fori_loop(0, RESP_DEV, own_part, 0, unroll=True)

    forward(0, 3, 6)
    forward(1, 3, 6)
    spread(0, 3)
    spread(1, 3)
    for sign in (1, -1):
        hop(0, sign, 0, 6).wait_recv()
    spread(0, 6)
    for sign in (1, -1):
        hop(1, sign, 0, 6).wait_recv()
    spread(1, 6)
    own()
    pltpu.make_async_copy(kb, kb, precv.at[0]).wait()

    def chosen(buf, j):
        rows = buf[pl.ds(2 * gids[first + j], 2)]
        return rows.astype(jnp.float32).reshape(PLEN, HD).astype(jnp.bfloat16)

    def keys_part(j, carry):
        s = lax.dot_general(stacked(j), chosen(kb, j), (((1,), (1,)), ((), ())), preferred_element_type=jnp.float32)
        m_own = m_s[j]
        m = jnp.maximum(m_own, jnp.max(s, axis=1, keepdims=True))
        mc = m * C2
        factor = jnp.exp2(m_own * C2 - mc)
        acc_s[j] = acc_s[j] * jnp.concatenate([factor, factor], axis=1)
        p_s[j] = jnp.exp2(s * C2 - jnp.concatenate([mc, mc], axis=1)).astype(jnp.bfloat16)
        return carry

    def values_part(j, carry):
        values = jnp.concatenate([chosen(vb, j), jnp.ones((PLEN, HD), jnp.bfloat16)], axis=1)
        acc = acc_s[j] + jnp.dot(p_s[j], values, preferred_element_type=jnp.float32)
        o = acc[:, :HD] / acc[:, HD:]
        live = lax.broadcasted_iota(jnp.int32, (RLEN, HD), 0) < lengths[first + j]
        for g in range(GROUP):
            part = jnp.where(live, o[g * RLEN : (g + 1) * RLEN], 0.0)
            obuf[pl.ds(j * RLEN, RLEN), g * HD : (g + 1) * HD] = part.astype(jnp.bfloat16)
        return carry

    lax.fori_loop(0, RESP_DEV, keys_part, 0, unroll=True)
    pltpu.make_async_copy(vb, vb, precv.at[1]).wait()
    lax.fori_loop(0, RESP_DEV, values_part, 0, unroll=True)
    for kv in range(2):
        for p, c in ((0, 3), (3, 6)):
            for sign in (1, -1):
                hop(kv, sign, p, c).wait_send()
    for kv in range(2):
        left = spread_count[0]
        while left:
            n = min(left, NZ * SLOTS)
            left -= n
            if n >= SLOTS:
                ref = kb.at[pl.ds(0, n // SLOTS)]
                pltpu.make_async_copy(ref, ref, psend.at[kv]).wait()
            if n % SLOTS:
                ref = kb.at[0, pl.ds(0, n % SLOTS)]
                pltpu.make_async_copy(ref, ref, psend.at[kv]).wait()
    ref = rb.at[pl.ds(0, 7)]
    pltpu.make_async_copy(ref, ref, rsend).wait()


def store(src, dst, sem):
    copy = pltpu.make_async_copy(src, dst, sem)
    copy.start()
    copy.wait()


def local(queries, response_kv, prompt_kv, group_ids, lengths, tree_parent):
    dma = pltpu.SemaphoreType.DMA
    anywhere = pl.BlockSpec(memory_space=pl.ANY)
    attended = pl.pallas_call(
        kernel,
        out_shape=pltpu.VMEM(queries.shape, jnp.bfloat16),
        in_specs=[anywhere] * 6,
        out_specs=pl.BlockSpec(memory_space=pltpu.VMEM),
        scratch_shapes=[
            pltpu.SMEM((RESPONSES,), jnp.int32),
            pltpu.SMEM((RESPONSES,), jnp.int32),
            pltpu.SMEM((NB, RESPONSES), jnp.int32),
            pltpu.VMEM((RESP_DEV * RLEN, GROUP * HD), jnp.bfloat16),
            pltpu.VMEM((NZ, LINE, KVH * HD), jnp.bfloat16),
            pltpu.VMEM((NZ, LINE, KVH * HD), jnp.bfloat16),
            pltpu.VMEM((NZ, SLOTS, LINE, HD), jnp.bfloat16),
            pltpu.VMEM((NZ, SLOTS, LINE, HD), jnp.bfloat16),
            pltpu.VMEM((8, 64, 2 * HD), jnp.bfloat16),
            pltpu.VMEM((RESP_DEV, GROUP * RLEN, 2 * HD), jnp.float32),
            pltpu.VMEM((RESP_DEV, GROUP * RLEN, HD), jnp.float32),
            pltpu.VMEM((RESP_DEV, GROUP * RLEN, PLEN), jnp.bfloat16),
            dma((2,)), dma((2,)), dma, dma, dma((2, 3, 9)), dma((2, 3, 9)), dma, dma((3,)), dma((2,)), pltpu.SemaphoreType.REGULAR,
        ],
        compiler_params=pltpu.CompilerParams(
            collective_id=0, has_side_effects=True, vmem_limit_bytes=60 << 20
        ),
        cost_estimate=pl.CostEstimate(flops=1 << 29, bytes_accessed=3 << 20, transcendentals=1 << 20),
    )(queries, response_kv, prompt_kv, group_ids, lengths, tree_parent.T)
    return pl.pallas_call(
        store,
        out_shape=jax.ShapeDtypeStruct(queries.shape, jnp.bfloat16),
        in_specs=[pl.BlockSpec(memory_space=pltpu.VMEM)],
        out_specs=anywhere,
        scratch_shapes=[dma],
        compiler_params=pltpu.CompilerParams(vmem_limit_bytes=2 << 20),
    )(attended)


def solution(mesh):
    placed = (
        P(("dp", "resp"), "tensor"),
        P(("dp", "resp", "tensor"), None),
        P(("dp", "resp", "tensor"), None),
        P("dp"),
        P("dp"),
        P("dp", None),
    )
    return jax.shard_map(
        local, mesh=mesh, in_specs=placed, out_specs=P(("dp", "resp"), "tensor"), check_vma=False
    )
```

```python
import math

import jax
import jax.numpy as jnp
from jax import lax
from jax.experimental import pallas as pl
from jax.experimental.pallas import tpu as pltpu
from jax.sharding import PartitionSpec as P

H = 40
KVH = 8
HD = 128
RLEN = 128
NB = 4
PLEN = 256
RESPONSES = 128
GROUP = H // KVH
RESP_DEV = 4
NZ = 16
SLOTS = 16
LINE = 8
NEG = -1e30
C2 = math.log2(math.e) / math.sqrt(HD)
MESH = pl.DeviceIdType.MESH
NEAR = (3, -3, 2, -2, 1, -1)


def own_mask(first, j, lengths, parents):
    length = lengths[first + j]
    p2 = parents[2, first + j]
    p3 = parents[3, first + j]
    s21 = p2 == 1
    s32 = p3 == 2
    s31 = (p3 == 1) | (s32 & s21)
    row = lax.broadcasted_iota(jnp.int32, (RLEN, RLEN), 0)
    col = lax.broadcasted_iota(jnp.int32, (RLEN, RLEN), 1)
    rb = row >> 5
    cb = col >> 5
    reach = jnp.where(rb == cb, row, -1)
    reach = jnp.where((cb == 0) & (rb > 0), RLEN, reach)
    reach = jnp.where((cb == 1) & (rb == 2), jnp.where(s21, RLEN, -1), reach)
    reach = jnp.where((cb == 1) & (rb == 3), jnp.where(s31, RLEN, -1), reach)
    reach = jnp.where((cb == 2) & (rb == 3), jnp.where(s32, RLEN, -1), reach)
    return (col <= reach) & (col < length)


def kernel(
    q_hbm, r_hbm, p_hbm, g_hbm, l_hbm, t_hbm, acc_s, p_s, v_s,
    gids, lengths, parents, qs, kr, vr, kb, vb, rb, m_s,
    psend, precv, rsend, rrecv, zsend, zrecv, qsem, ssem, lsem, ready,
):
    resp = lax.axis_index("resp")
    t = lax.axis_index("tensor")
    z = resp // 2
    xh = resp % 2
    first = resp * RESP_DEV
    slot = xh * 8 + t

    def zz(o):
        return (z + o + NZ) % NZ

    def place(r, tt):
        return {"resp": r, "tensor": tt}

    def remote(src, dst, ss, rs, r, tt):
        return pltpu.make_async_remote_copy(
            src_ref=src, dst_ref=dst, send_sem=ss, recv_sem=rs, device_id=place(r, tt), device_id_type=MESH
        )

    peers = sorted(
        ((k // 8, k % 8) for k in range(1, SLOTS)), key=lambda p: (-2 * p[0] - min(p[1] // 2, 4 - p[1] // 2) - p[1] % 2, p)
    )

    def greet(sem, r, tt):
        pl.semaphore_signal(sem, inc=1, device_id=place(r, tt), device_id_type=MESH)

    barrier = pltpu.get_barrier_semaphore()
    for o in NEAR:
        greet(barrier, zz(o) * 2 + xh, t)
    for dx, dt in peers:
        greet(barrier, z * 2 + (xh + dx) % 2, (t + dt) % 8)

    raws = (kr, vr)
    for kv in range(2):
        for h in range(KVH):
            pltpu.make_async_copy(
                p_hbm.at[:, pl.ds((2 * h + kv) * HD, HD)], raws[kv].at[z, :, pl.ds(h * HD, HD)], lsem.at[kv]
            ).start()
    small = [
        pltpu.make_async_copy(src, dst, ssem.at[i])
        for i, (src, dst) in enumerate(((g_hbm, gids), (l_hbm, lengths), (t_hbm, parents)))
    ]
    for copy in small:
        copy.start()
    q_copy = pltpu.make_async_copy(q_hbm, qs, qsem)
    q_copy.start()

    for kv in range(2):
        pltpu.make_async_copy(raws[kv].at[z], raws[kv].at[z], lsem.at[kv]).wait()
    pl.semaphore_wait(barrier, len(NEAR) + len(peers))

    def pair(tt):
        return pl.ds(pl.multiple_of(tt * (2 * HD), 2 * HD), 2 * HD)

    def hop(kv, sign, p, c):
        ref = raws[kv].at[zz(-sign * p)]
        return remote(
            ref, ref, zsend.at[kv, sign % 3, c], zrecv.at[kv, sign % 3, c], zz(sign * (c - p)) * 2 + xh, t
        )

    def forward(kv, p, c):
        for sign in (1, -1):
            if p:
                hop(kv, sign, 0, p).wait_recv()
            hop(kv, sign, p, c).start()

    spread_count = [0]

    def column(tt):
        return pl.ds(pl.multiple_of(tt * HD, HD), HD)

    def to_plane(src, o, half=None, kvs=(0, 1)):
        targets = peers if o == 0 else peers + [(0, 0)]
        for kv in kvs:
            buf = (kb, vb)[kv]
            for dx, dt in targets:
                if half is not None and dx:
                    continue
                tt = (t + dt) % 8
                r = zz(o) * 2 + (half if half is not None else (xh + dx) % 2)
                remote(raws[kv].at[src, :, column(tt)], buf.at[src, slot], psend.at[kv], precv.at[kv], r, tt).start()
                if kv == 0:
                    spread_count[0] += 1
            if o == 0:
                pltpu.make_async_copy(raws[kv].at[src, :, column(t)], buf.at[src, slot], precv.at[kv]).start()

    def spread(kv, c):
        for sign in (1, -1):
            src = zz(-c * sign)
            if c == 6:
                to_plane(src, 2 * sign, 0 if sign == 1 else 1, (kv,))
            for o in (1, -1, 0):
                to_plane(src, o, None, (kv,))

    forward(0, 0, 3)
    forward(1, 0, 3)
    for dx, dt in peers:
        greet(ready, z * 2 + (xh + dx) % 2, (t + dt) % 8)
    to_plane(z, 0)

    pltpu.make_async_copy(r_hbm.at[:, pair(t)], rb.at[t], rrecv).start()
    for dt in range(1, 8):
        tt = (t + dt) % 8
        remote(r_hbm.at[:, pair(tt)], rb.at[t], rsend, rrecv, resp, tt).start()

    pl.semaphore_wait(ready, len(peers))
    to_plane(z, 1)
    to_plane(z, -1)

    for copy in small:
        copy.wait()
    q_copy.wait()

    def stacked(j):
        rows = qs[pl.ds(j * RLEN, RLEN), :]
        return jnp.concatenate([rows[:, g * HD : (g + 1) * HD] for g in range(GROUP)], axis=0)

    def own_part(j, carry):
        rows = rb[pl.ds(2 * j, 2)].reshape(RLEN, 2 * HD)
        keys = rows[:, :HD]
        values = jnp.concatenate([rows[:, HD:], jnp.ones((RLEN, HD), jnp.bfloat16)], axis=1)
        bias = jnp.where(own_mask(first, j, lengths, parents), 0.0, NEG)
        s = lax.dot_general(stacked(j), keys, (((1,), (1,)), ((), ())), preferred_element_type=jnp.float32)
        s = s + jnp.concatenate([bias] * GROUP, axis=0)
        m = jnp.max(s, axis=1, keepdims=True)
        e = jnp.exp2(s * C2 - m * C2).astype(jnp.bfloat16)
        acc_s[j] = jnp.dot(e, values, preferred_element_type=jnp.float32)
        m_s[j] = jnp.broadcast_to(m, (GROUP * RLEN, HD))
        return carry

    def own():
        pltpu.make_async_copy(rb, rb, rrecv).wait()
        lax.fori_loop(0, RESP_DEV, own_part, 0, unroll=True)

    forward(0, 3, 6)
    forward(1, 3, 6)
    spread(0, 3)
    spread(1, 3)
    for sign in (1, -1):
        hop(0, sign, 0, 6).wait_recv()
    spread(0, 6)
    for sign in (1, -1):
        hop(1, sign, 0, 6).wait_recv()
    spread(1, 6)
    own()
    pltpu.make_async_copy(kb, kb, precv.at[0]).wait()

    def chosen(buf, j):
        rows = buf[pl.ds(2 * gids[first + j], 2)]
        return rows.astype(jnp.float32).reshape(PLEN, HD).astype(jnp.bfloat16)

    def keys_part(j, carry):
        s = lax.dot_general(stacked(j), chosen(kb, j), (((1,), (1,)), ((), ())), preferred_element_type=jnp.float32)
        m_own = m_s[j]
        m = jnp.maximum(m_own, jnp.max(s, axis=1, keepdims=True))
        live = lax.broadcasted_iota(jnp.int32, (RLEN, HD), 0) < lengths[first + j]
        mc = m * C2 + jnp.concatenate([jnp.where(live, 0.0, -NEG)] * GROUP, axis=0)
        factor = jnp.exp2(m_own * C2 - mc)
        acc_s[j] = acc_s[j] * jnp.concatenate([factor, factor], axis=1)
        p_s[j] = jnp.exp2(s * C2 - jnp.concatenate([mc, mc], axis=1)).astype(jnp.bfloat16)
        return carry

    lax.fori_loop(0, RESP_DEV, keys_part, 0, unroll=True)
    pltpu.make_async_copy(vb, vb, precv.at[1]).wait()
    for j in range(RESP_DEV):
        v_s[j] = chosen(vb, j)
    for kv in range(2):
        for p, c in ((0, 3), (3, 6)):
            for sign in (1, -1):
                hop(kv, sign, p, c).wait_send()
    for kv in range(2):
        left = spread_count[0]
        while left:
            n = min(left, NZ * SLOTS)
            left -= n
            if n >= SLOTS:
                ref = kb.at[pl.ds(0, n // SLOTS)]
                pltpu.make_async_copy(ref, ref, psend.at[kv]).wait()
            if n % SLOTS:
                ref = kb.at[0, pl.ds(0, n % SLOTS)]
                pltpu.make_async_copy(ref, ref, psend.at[kv]).wait()
    ref = rb.at[pl.ds(0, 7)]
    pltpu.make_async_copy(ref, ref, rsend).wait()


def weigh(own, weights, rows, out, buf, sem):
    def copy(j):
        part = pl.ds(j * RLEN, RLEN)
        return pltpu.make_async_copy(buf.at[part], out.at[part], sem.at[j])

    for j in range(RESP_DEV):
        values = jnp.concatenate([rows[j], jnp.ones((PLEN, HD), jnp.bfloat16)], axis=1)
        acc = own[j] + jnp.dot(weights[j], values, preferred_element_type=jnp.float32)
        o = (acc[:, :HD] / jnp.maximum(acc[:, HD:], 1.0)).astype(jnp.bfloat16)
        for g in range(GROUP):
            buf[j * RLEN : (j + 1) * RLEN, g * HD : (g + 1) * HD] = o[g * RLEN : (g + 1) * RLEN]
        copy(j).start()
    for j in range(RESP_DEV):
        copy(j).wait()


def local(queries, response_kv, prompt_kv, group_ids, lengths, tree_parent):
    dma = pltpu.SemaphoreType.DMA
    anywhere = pl.BlockSpec(memory_space=pl.ANY)
    parts = pl.pallas_call(
        kernel,
        out_shape=(
            pltpu.VMEM((RESP_DEV, GROUP * RLEN, 2 * HD), jnp.float32),
            pltpu.VMEM((RESP_DEV, GROUP * RLEN, PLEN), jnp.bfloat16),
            pltpu.VMEM((RESP_DEV, PLEN, HD), jnp.bfloat16),
        ),
        in_specs=[anywhere] * 6,
        out_specs=(pl.BlockSpec(memory_space=pltpu.VMEM),) * 3,
        scratch_shapes=[
            pltpu.SMEM((RESPONSES,), jnp.int32),
            pltpu.SMEM((RESPONSES,), jnp.int32),
            pltpu.SMEM((NB, RESPONSES), jnp.int32),
            pltpu.VMEM((RESP_DEV * RLEN, GROUP * HD), jnp.bfloat16),
            pltpu.VMEM((NZ, LINE, KVH * HD), jnp.bfloat16),
            pltpu.VMEM((NZ, LINE, KVH * HD), jnp.bfloat16),
            pltpu.VMEM((NZ, SLOTS, LINE, HD), jnp.bfloat16),
            pltpu.VMEM((NZ, SLOTS, LINE, HD), jnp.bfloat16),
            pltpu.VMEM((8, 64, 2 * HD), jnp.bfloat16),
            pltpu.VMEM((RESP_DEV, GROUP * RLEN, HD), jnp.float32),
            dma((2,)), dma((2,)), dma, dma, dma((2, 3, 9)), dma((2, 3, 9)), dma, dma((3,)), dma((2,)), pltpu.SemaphoreType.REGULAR,
        ],
        compiler_params=pltpu.CompilerParams(
            collective_id=0, has_side_effects=True, vmem_limit_bytes=56 << 20
        ),
        cost_estimate=pl.CostEstimate(flops=1 << 29, bytes_accessed=3 << 20, transcendentals=1 << 20),
    )(queries, response_kv, prompt_kv, group_ids, lengths, tree_parent.T)
    return pl.pallas_call(
        weigh,
        out_shape=jax.ShapeDtypeStruct(queries.shape, jnp.bfloat16),
        in_specs=[pl.BlockSpec(memory_space=pltpu.VMEM)] * 3,
        out_specs=anywhere,
        scratch_shapes=[pltpu.VMEM(queries.shape, jnp.bfloat16), dma((RESP_DEV,))],
        compiler_params=pltpu.CompilerParams(vmem_limit_bytes=8 << 20),
    )(*parts)


def solution(mesh):
    placed = (
        P(("dp", "resp"), "tensor"),
        P(("dp", "resp", "tensor"), None),
        P(("dp", "resp", "tensor"), None),
        P("dp"),
        P("dp"),
        P("dp", None),
    )
    return jax.shard_map(
        local, mesh=mesh, in_specs=placed, out_specs=P(("dp", "resp"), "tensor"), check_vma=False
    )
```

```python
import math

import jax
import jax.numpy as jnp
from jax import lax
from jax.experimental import pallas as pl
from jax.experimental.pallas import tpu as pltpu
from jax.sharding import PartitionSpec as P

H = 40
KVH = 8
HD = 128
RLEN = 128
NB = 4
PLEN = 256
RESPONSES = 128
GROUP = H // KVH
RESP_DEV = 4
NZ = 16
SLOTS = 16
LINE = 8
NEG = -1e30
C2 = math.log2(math.e) / math.sqrt(HD)
MESH = pl.DeviceIdType.MESH
NEAR = (3, -3, 2, -2, 1, -1)


def own_mask(first, j, lengths, parents):
    length = lengths[first + j]
    p2 = parents[2, first + j]
    p3 = parents[3, first + j]
    s21 = p2 == 1
    s32 = p3 == 2
    s31 = (p3 == 1) | (s32 & s21)
    row = lax.broadcasted_iota(jnp.int32, (RLEN, RLEN), 0)
    col = lax.broadcasted_iota(jnp.int32, (RLEN, RLEN), 1)
    rb = row >> 5
    cb = col >> 5
    reach = jnp.where(rb == cb, row, -1)
    reach = jnp.where((cb == 0) & (rb > 0), RLEN, reach)
    reach = jnp.where((cb == 1) & (rb == 2), jnp.where(s21, RLEN, -1), reach)
    reach = jnp.where((cb == 1) & (rb == 3), jnp.where(s31, RLEN, -1), reach)
    reach = jnp.where((cb == 2) & (rb == 3), jnp.where(s32, RLEN, -1), reach)
    return (col <= reach) & (col < length)


def kernel(
    q_hbm, r_hbm, p_hbm, g_hbm, l_hbm, t_hbm, acc_s, p_s, v_s,
    gids, lengths, parents, qs, kr, vr, kb, vb, rb, m_s,
    psend, precv, rsend, rrecv, zsend, zrecv, qsem, ssem, lsem, ready,
):
    resp = lax.axis_index("resp")
    t = lax.axis_index("tensor")
    z = resp // 2
    xh = resp % 2
    first = resp * RESP_DEV
    slot = xh * 8 + t

    def zz(o):
        return (z + o + NZ) % NZ

    def place(r, tt):
        return {"resp": r, "tensor": tt}

    def remote(src, dst, ss, rs, r, tt):
        return pltpu.make_async_remote_copy(
            src_ref=src, dst_ref=dst, send_sem=ss, recv_sem=rs, device_id=place(r, tt), device_id_type=MESH
        )

    peers = sorted(
        ((k // 8, k % 8) for k in range(1, SLOTS)), key=lambda p: (-2 * p[0] - min(p[1] // 2, 4 - p[1] // 2) - p[1] % 2, p)
    )

    def greet(sem, r, tt):
        pl.semaphore_signal(sem, inc=1, device_id=place(r, tt), device_id_type=MESH)

    barrier = pltpu.get_barrier_semaphore()
    for o in NEAR:
        greet(barrier, zz(o) * 2 + xh, t)
    for dx, dt in peers:
        greet(barrier, z * 2 + (xh + dx) % 2, (t + dt) % 8)

    raws = (kr, vr)
    for kv in range(2):
        for h in range(KVH):
            pltpu.make_async_copy(
                p_hbm.at[:, pl.ds((2 * h + kv) * HD, HD)], raws[kv].at[z, :, pl.ds(h * HD, HD)], lsem.at[kv]
            ).start()
    small = [
        pltpu.make_async_copy(src, dst, ssem.at[i])
        for i, (src, dst) in enumerate(((g_hbm, gids), (l_hbm, lengths), (t_hbm, parents)))
    ]
    for copy in small:
        copy.start()
    q_copy = pltpu.make_async_copy(q_hbm, qs, qsem)
    q_copy.start()

    for kv in range(2):
        pltpu.make_async_copy(raws[kv].at[z], raws[kv].at[z], lsem.at[kv]).wait()
    pl.semaphore_wait(barrier, len(NEAR) + len(peers))

    def pair(tt):
        return pl.ds(pl.multiple_of(tt * (2 * HD), 2 * HD), 2 * HD)

    def hop(kv, sign, p, c):
        ref = raws[kv].at[zz(-sign * p)]
        return remote(
            ref, ref, zsend.at[kv, sign % 3, c], zrecv.at[kv, sign % 3, c], zz(sign * (c - p)) * 2 + xh, t
        )

    def forward(kv, p, c):
        for sign in (1, -1):
            if p:
                hop(kv, sign, 0, p).wait_recv()
            hop(kv, sign, p, c).start()

    spread_count = [0]

    def column(tt):
        return pl.ds(pl.multiple_of(tt * HD, HD), HD)

    def to_plane(src, o, half=None, kvs=(0, 1)):
        targets = peers if o == 0 else peers + [(0, 0)]
        for kv in kvs:
            buf = (kb, vb)[kv]
            for dx, dt in targets:
                if half is not None and dx:
                    continue
                tt = (t + dt) % 8
                r = zz(o) * 2 + (half if half is not None else (xh + dx) % 2)
                remote(raws[kv].at[src, :, column(tt)], buf.at[src, slot], psend.at[kv], precv.at[kv], r, tt).start()
                if kv == 0:
                    spread_count[0] += 1
            if o == 0:
                pltpu.make_async_copy(raws[kv].at[src, :, column(t)], buf.at[src, slot], precv.at[kv]).start()

    def spread(kv, c):
        for sign in (1, -1):
            src = zz(-c * sign)
            if c == 6:
                to_plane(src, 2 * sign, 0 if sign == 1 else 1, (kv,))
        for o in (0, 1, -1):
            for sign in (1, -1):
                to_plane(zz(-c * sign), o * sign, None, (kv,))

    forward(0, 0, 3)
    forward(1, 0, 3)
    for dx, dt in peers:
        greet(ready, z * 2 + (xh + dx) % 2, (t + dt) % 8)
    to_plane(z, 0)

    pltpu.make_async_copy(r_hbm.at[:, pair(t)], rb.at[t], rrecv).start()
    for dt in range(1, 8):
        tt = (t + dt) % 8
        remote(r_hbm.at[:, pair(tt)], rb.at[t], rsend, rrecv, resp, tt).start()

    pl.semaphore_wait(ready, len(peers))
    to_plane(z, 1)
    to_plane(z, -1)

    for copy in small:
        copy.wait()
    q_copy.wait()

    def stacked(j):
        rows = qs[pl.ds(j * RLEN, RLEN), :]
        return jnp.concatenate([rows[:, g * HD : (g + 1) * HD] for g in range(GROUP)], axis=0)

    def own_part(j, carry):
        rows = rb[pl.ds(2 * j, 2)].reshape(RLEN, 2 * HD)
        keys = rows[:, :HD]
        values = jnp.concatenate([rows[:, HD:], jnp.ones((RLEN, HD), jnp.bfloat16)], axis=1)
        bias = jnp.where(own_mask(first, j, lengths, parents), 0.0, NEG)
        s = lax.dot_general(stacked(j), keys, (((1,), (1,)), ((), ())), preferred_element_type=jnp.float32)
        s = s + jnp.concatenate([bias] * GROUP, axis=0)
        m = jnp.max(s, axis=1, keepdims=True)
        e = jnp.exp2(s * C2 - m * C2).astype(jnp.bfloat16)
        acc_s[j] = jnp.dot(e, values, preferred_element_type=jnp.float32)
        m_s[j] = jnp.broadcast_to(m, (GROUP * RLEN, HD))
        return carry

    def own():
        pltpu.make_async_copy(rb, rb, rrecv).wait()
        lax.fori_loop(0, RESP_DEV, own_part, 0, unroll=True)

    forward(0, 3, 6)
    forward(1, 3, 6)
    spread(0, 3)
    spread(1, 3)
    for sign in (1, -1):
        hop(0, sign, 0, 6).wait_recv()
    spread(0, 6)
    for sign in (1, -1):
        hop(1, sign, 0, 6).wait_recv()
    spread(1, 6)
    own()
    pltpu.make_async_copy(kb, kb, precv.at[0]).wait()

    def chosen(buf, j):
        rows = buf[pl.ds(2 * gids[first + j], 2)]
        return rows.astype(jnp.float32).reshape(PLEN, HD).astype(jnp.bfloat16)

    def keys_part(j, carry):
        s = lax.dot_general(stacked(j), chosen(kb, j), (((1,), (1,)), ((), ())), preferred_element_type=jnp.float32)
        m_own = m_s[j]
        m = jnp.maximum(m_own, jnp.max(s, axis=1, keepdims=True))
        live = lax.broadcasted_iota(jnp.int32, (RLEN, HD), 0) < lengths[first + j]
        mc = m * C2 + jnp.concatenate([jnp.where(live, 0.0, -NEG)] * GROUP, axis=0)
        factor = jnp.exp2(m_own * C2 - mc)
        acc_s[j] = acc_s[j] * jnp.concatenate([factor, factor], axis=1)
        p_s[j] = jnp.exp2(s * C2 - jnp.concatenate([mc, mc], axis=1)).astype(jnp.bfloat16)
        return carry

    lax.fori_loop(0, RESP_DEV, keys_part, 0, unroll=True)
    pltpu.make_async_copy(vb, vb, precv.at[1]).wait()
    for j in range(RESP_DEV):
        v_s[j] = chosen(vb, j)
    for kv in range(2):
        for p, c in ((0, 3), (3, 6)):
            for sign in (1, -1):
                hop(kv, sign, p, c).wait_send()
    for kv in range(2):
        left = spread_count[0]
        while left:
            n = min(left, NZ * SLOTS)
            left -= n
            if n >= SLOTS:
                ref = kb.at[pl.ds(0, n // SLOTS)]
                pltpu.make_async_copy(ref, ref, psend.at[kv]).wait()
            if n % SLOTS:
                ref = kb.at[0, pl.ds(0, n % SLOTS)]
                pltpu.make_async_copy(ref, ref, psend.at[kv]).wait()
    ref = rb.at[pl.ds(0, 7)]
    pltpu.make_async_copy(ref, ref, rsend).wait()


def weigh(own, weights, rows, out, buf, sem):
    def copy(j):
        part = pl.ds(j * RLEN, RLEN)
        return pltpu.make_async_copy(buf.at[part], out.at[part], sem.at[j])

    for j in range(RESP_DEV):
        values = jnp.concatenate([rows[j], jnp.ones((PLEN, HD), jnp.bfloat16)], axis=1)
        acc = own[j] + jnp.dot(weights[j], values, preferred_element_type=jnp.float32)
        o = (acc[:, :HD] / jnp.maximum(acc[:, HD:], 1.0)).astype(jnp.bfloat16)
        for g in range(GROUP):
            buf[j * RLEN : (j + 1) * RLEN, g * HD : (g + 1) * HD] = o[g * RLEN : (g + 1) * RLEN]
        copy(j).start()
    for j in range(RESP_DEV):
        copy(j).wait()


def local(queries, response_kv, prompt_kv, group_ids, lengths, tree_parent):
    dma = pltpu.SemaphoreType.DMA
    anywhere = pl.BlockSpec(memory_space=pl.ANY)
    parts = pl.pallas_call(
        kernel,
        out_shape=(
            pltpu.VMEM((RESP_DEV, GROUP * RLEN, 2 * HD), jnp.float32),
            pltpu.VMEM((RESP_DEV, GROUP * RLEN, PLEN), jnp.bfloat16),
            pltpu.VMEM((RESP_DEV, PLEN, HD), jnp.bfloat16),
        ),
        in_specs=[anywhere] * 6,
        out_specs=(pl.BlockSpec(memory_space=pltpu.VMEM),) * 3,
        scratch_shapes=[
            pltpu.SMEM((RESPONSES,), jnp.int32),
            pltpu.SMEM((RESPONSES,), jnp.int32),
            pltpu.SMEM((NB, RESPONSES), jnp.int32),
            pltpu.VMEM((RESP_DEV * RLEN, GROUP * HD), jnp.bfloat16),
            pltpu.VMEM((NZ, LINE, KVH * HD), jnp.bfloat16),
            pltpu.VMEM((NZ, LINE, KVH * HD), jnp.bfloat16),
            pltpu.VMEM((NZ, SLOTS, LINE, HD), jnp.bfloat16),
            pltpu.VMEM((NZ, SLOTS, LINE, HD), jnp.bfloat16),
            pltpu.VMEM((8, 64, 2 * HD), jnp.bfloat16),
            pltpu.VMEM((RESP_DEV, GROUP * RLEN, HD), jnp.float32),
            dma((2,)), dma((2,)), dma, dma, dma((2, 3, 9)), dma((2, 3, 9)), dma, dma((3,)), dma((2,)), pltpu.SemaphoreType.REGULAR,
        ],
        compiler_params=pltpu.CompilerParams(
            collective_id=0, has_side_effects=True, vmem_limit_bytes=56 << 20
        ),
        cost_estimate=pl.CostEstimate(flops=1 << 29, bytes_accessed=3 << 20, transcendentals=1 << 20),
    )(queries, response_kv, prompt_kv, group_ids, lengths, tree_parent.T)
    return pl.pallas_call(
        weigh,
        out_shape=jax.ShapeDtypeStruct(queries.shape, jnp.bfloat16),
        in_specs=[pl.BlockSpec(memory_space=pltpu.VMEM)] * 3,
        out_specs=anywhere,
        scratch_shapes=[pltpu.VMEM(queries.shape, jnp.bfloat16), dma((RESP_DEV,))],
        compiler_params=pltpu.CompilerParams(vmem_limit_bytes=8 << 20),
    )(*parts)


def solution(mesh):
    placed = (
        P(("dp", "resp"), "tensor"),
        P(("dp", "resp", "tensor"), None),
        P(("dp", "resp", "tensor"), None),
        P("dp"),
        P("dp"),
        P("dp", None),
    )
    return jax.shard_map(
        local, mesh=mesh, in_specs=placed, out_specs=P(("dp", "resp"), "tensor"), check_vma=False
    )
```
